32 devices in a mesh: grp: 2 (over x), frame: 16 (over z, y, core).
Axes of the slice: x: 2, y: 2, z: 4, core: 2. Of those that a mesh axis runs over, the one named last changes fastest.
Arguments:
- mixer_input: bfloat16 [8192, 2048], P(('grp', 'frame')), parts along dimension 0, may hold values from -6 to 6
- state_input: bfloat16 [8192, 128], P(('grp', 'frame')), parts along dimension 0, may hold values from -0.08984375 to 0.08984375
- state_output: bfloat16 [8192, 128], P(('grp', 'frame')), parts along dimension 0, may hold values from -0.08984375 to 0.08984375
- log_decay: float32 [8192, 32], P(('grp', 'frame')), parts along dimension 0, may hold values from -1 to 0
- queries: bfloat16 [8192, 2048], P(('grp', 'frame')), parts along dimension 0, may hold values from -6 to 6
- attn_keys: bfloat16 [8192, 2048], P(('grp', 'frame')), parts along dimension 0, may hold values from -6 to 6
- out_grad: bfloat16 [8192, 2048], P(('grp', 'frame')), parts along dimension 0, may hold values from -6 to 6
- frame_offsets: int32 [64], P('grp'), parts along dimension 0, may hold values from 1 to 2, as said below
- sink_frame_index: int32 [2], P('grp'), parts along dimension 0, may hold values from 0 to 31
Outputs:
- grad_input: bfloat16 [8192, 2048], P(('grp', 'frame')), parts along dimension 0
- grad_queries: bfloat16 [8192, 2048], P(('grp', 'frame')), parts along dimension 0
- grad_keys: bfloat16 [8192, 2048], P(('grp', 'frame')), parts along dimension 0
- grad_state_input: float32 [8192, 128], P(('grp', 'frame')), parts along dimension 0
- grad_state_output: float32 [8192, 128], P(('grp', 'frame')), parts along dimension 0
The draws below stay inside these ranges and needn't reach their ends.
There are 2 independent parts, one for each index of `grp`. The reference program is written for one: setup_inputs(seed, part) draws one part's arguments, and reference() takes and returns one part's arrays. A program takes and returns all parts, laid end to end along the dimension named above; each array names one. Nothing has to cross between parts.
Inputs may be any that keep to these rules, and one draw needn't show every extreme that they name: `frame_offsets`: both 1 and 2 occur in every clip.
All inputs are finite; a program needn't handle non-finite values.
Results may differ from the reference program's by a relative error of at most 0.0095.
Values may be sent and summed in bfloat16 or wider, within the bound.
A program may use at most 256 MiB of HBM per device.

```python
import math
import jax
import jax.numpy as jnp
from jax import lax

DI = 2048
HEADDIM = 64
NSTATE = 128
ATTENTION_WIDTH = 128
S = 128
OFFMAX = 2
HEADS = 32
NF = 32
VIDEO_SPAN_ITEMS = 4096


def query_key_pair(key):
    base_key = jax.random.fold_in(key, 7)
    split_lookup_vectors = jax.random.split(base_key, 2)
    raw_q = jnp.clip(jax.random.normal(split_lookup_vectors[0], (VIDEO_SPAN_ITEMS, DI), jnp.float32), -6.0, 6.0)
    raw_k = jnp.clip(jax.random.normal(split_lookup_vectors[1], (VIDEO_SPAN_ITEMS, DI), jnp.float32), -6.0, 6.0)
    return (raw_q, raw_k)


def draw_queries(key, part):
    return query_key_pair(key)[0].astype(jnp.bfloat16)


def draw_attn_keys(key, part):
    return query_key_pair(key)[1].astype(jnp.bfloat16)


def head_rates(key):
    split_lookup_vectors = jax.random.split(jax.random.fold_in(key, 11), 4)
    strata = jax.random.permutation(split_lookup_vectors[0], HEADS)
    fast_count = HEADS // 4
    medium_count = max(1, HEADS // 4)
    slow_rate = math.log(10.0) / VIDEO_SPAN_ITEMS * jnp.exp(jax.random.uniform(split_lookup_vectors[1], (HEADS,), jnp.float32, math.log(0.03), math.log(0.15)))
    fast_rate = 3.0 / jax.random.uniform(split_lookup_vectors[2], (HEADS,), jnp.float32, 30.0, 50.0)
    location_slot = (strata.astype(jnp.float32) - fast_count + jax.random.uniform(split_lookup_vectors[3], (HEADS,), jnp.float32)) / medium_count
    location_slot = jnp.clip(location_slot, 0.0, 1.0)
    medium_rate = 0.0055 * jnp.exp(location_slot * math.log(0.013 / 0.0055))
    return jnp.where(strata < fast_count, fast_rate, jnp.where(strata < fast_count + medium_count, medium_rate, slow_rate))


def channel_gain(key):
    head_gain = jnp.clip((head_rates(key) / 0.006) ** 0.25, 0.3, 1.0)
    return jnp.repeat(head_gain, HEADDIM)


def scaled_activity(key, salt):
    split_lookup_vectors = jax.random.split(jax.random.fold_in(key, salt), 2)
    raw_values = jnp.clip(jax.random.normal(split_lookup_vectors[0], (VIDEO_SPAN_ITEMS, DI), jnp.float32), -6.0, 6.0)
    frame_level = jnp.exp(jax.random.uniform(split_lookup_vectors[1], (NF, 1), jnp.float32, -3.5, 0.0))
    frame_level = jnp.repeat(frame_level, S, axis=0)
    return raw_values * frame_level * channel_gain(key)[None, :]


def draw_mixer_input(key, part):
    return scaled_activity(key, 13).astype(jnp.bfloat16)


def draw_out_grad(key, part):
    return scaled_activity(key, 17).astype(jnp.bfloat16)


def draw_log_decay(key, part):
    split_lookup_vectors = jax.random.split(jax.random.fold_in(key, 3), 3)
    channel_speed_each = head_rates(key)
    scaling_factor = jnp.exp(jax.random.uniform(split_lookup_vectors[0], (NF, 1), jnp.float32, -math.log(2.0), math.log(2.0)))
    scaling_factor = jnp.repeat(scaling_factor, S, axis=0)
    spike_position = jax.random.randint(split_lookup_vectors[1], (3,), 0, VIDEO_SPAN_ITEMS)
    token_positions = jnp.arange(VIDEO_SPAN_ITEMS, dtype=jnp.int32)
    equality_flag = jnp.any(token_positions[:, None] == spike_position[None, :], axis=1)
    spike_cost_weight = jnp.log(jax.random.uniform(split_lookup_vectors[2], (VIDEO_SPAN_ITEMS, 1), jnp.float32, 0.6, 0.8))
    return -(channel_speed_each[None, :] * scaling_factor) + jnp.where(equality_flag[:, None], spike_cost_weight, 0.0)


def draw_frame_offsets(key, part):
    split_lookup_vectors = jax.random.split(jax.random.fold_in(key, 5), 3)
    offsets = jax.random.randint(split_lookup_vectors[0], (NF,), 1, OFFMAX + 1)
    first_spot = jax.random.randint(split_lookup_vectors[1], (), 0, NF)
    second_spot = (first_spot + jax.random.randint(split_lookup_vectors[2], (), 1, NF)) % NF
    token_positions = jnp.arange(NF, dtype=jnp.int32)
    offsets = jnp.where(token_positions == first_spot, OFFMAX, offsets)
    offsets = jnp.where(token_positions == second_spot, 1, offsets)
    return offsets.astype(jnp.int32)


def shard_levels(rng, extent, cuts, smallest, largest):
    def one(position, parts):
        heights = jax.random.uniform(jax.random.fold_in(jax.random.fold_in(rng, 6), position), (parts,), jnp.float32, smallest / len(cuts), largest / len(cuts))
        return jnp.repeat(jnp.exp(heights), extent[position] // parts).reshape((-1,) + (1,) * (len(extent) - position - 1))

    loudness = one(*cuts[0])
    for cut in cuts[1:]:
        loudness = loudness * one(*cut)
    return loudness


def bell_draw(rng, extent, scale, bound, cuts=(), held_as=jnp.bfloat16):
    level = shard_levels(rng, extent, cuts, -0.22, 0.18) if cuts else 1.0
    array = jax.random.normal(rng, extent, jnp.float32) * scale * level
    return jnp.minimum(jnp.maximum(array, -bound), bound).astype(held_as)


def setup_inputs(seed: int = 0, part: int = 0) -> dict:
    streams_of = jax.random.split(jax.random.key(seed), 10)
    part_splits = jax.random.split(jax.random.fold_in(streams_of[9], part), 10)
    return {
        "mixer_input": draw_mixer_input(jax.random.fold_in(jax.random.fold_in(streams_of[9], part), 71), part),
        "state_input": bell_draw(part_splits[1], (VIDEO_SPAN_ITEMS, NSTATE), 0.015, 0.08984375, ((0, 16),)),
        "state_output": bell_draw(part_splits[2], (VIDEO_SPAN_ITEMS, NSTATE), 0.015, 0.08984375, ((0, 16),)),
        "log_decay": draw_log_decay(jax.random.fold_in(jax.random.fold_in(streams_of[9], part), 71), part),
        "queries": draw_queries(jax.random.fold_in(jax.random.fold_in(streams_of[9], part), 71), part),
        "attn_keys": draw_attn_keys(jax.random.fold_in(jax.random.fold_in(streams_of[9], part), 71), part),
        "out_grad": draw_out_grad(jax.random.fold_in(jax.random.fold_in(streams_of[9], part), 71), part),
        "frame_offsets": draw_frame_offsets(jax.random.fold_in(jax.random.fold_in(streams_of[9], part), 71), part),
        "sink_frame_index": jax.random.randint(part_splits[8], (1,), 0, NF).astype(jnp.int32),
    }


highest = lax.Precision.HIGHEST


def block_parts(x_block, b_block, c_block, decay_block, dout_block):
    head_count = DI // HEADDIM
    cumulative = jnp.cumsum(decay_block, axis=0)
    ending = cumulative[-1]
    to_end = jnp.exp(ending[None, :] - cumulative)
    x_heads = x_block.astype(jnp.float32).reshape(S, head_count, HEADDIM)
    d_heads = dout_block.astype(jnp.float32).reshape(S, head_count, HEADDIM)
    state_part = jnp.einsum('shp,sn->hpn', to_end[:, :, None] * x_heads, b_block.astype(jnp.float32), precision=highest)
    partial_gradient = jnp.einsum('shp,sn->hpn', jnp.exp(cumulative)[:, :, None] * d_heads, c_block.astype(jnp.float32), precision=highest)
    return state_part, partial_gradient, ending


def block_grads(x_block, b_block, c_block, decay_block, dout_block, state_before, grad_after):
    head_count = DI // HEADDIM
    cumulative = jnp.cumsum(decay_block, axis=0)
    ending = cumulative[-1]
    token_positions = jnp.arange(S, dtype=jnp.int32)
    lower = (token_positions[:, None] >= token_positions[None, :])[None]
    spread = cumulative.T[:, :, None] - cumulative.T[:, None, :]
    weights = jnp.where(lower, jnp.exp(jnp.where(lower, spread, 0.0)), 0.0)
    inner_cb = jnp.dot(c_block, b_block.T, preferred_element_type=jnp.float32)
    mixing = lax.optimization_barrier((weights * inner_cb[None]).astype(jnp.bfloat16)).astype(jnp.float32)
    x_heads = x_block.astype(jnp.float32).reshape(S, head_count, HEADDIM)
    d_heads = dout_block.astype(jnp.float32).reshape(S, head_count, HEADDIM)
    dx_inner = jnp.einsum('hts,thp->shp', mixing, d_heads)
    pair_dots = jnp.einsum('thp,shp->hts', d_heads, x_heads)
    folded = jnp.sum(weights * pair_dots, axis=0).astype(jnp.bfloat16)
    grad_b = jnp.dot(folded.T, c_block, preferred_element_type=jnp.float32)
    grad_c = jnp.dot(folded, b_block, preferred_element_type=jnp.float32)
    to_end = jnp.exp(ending[None, :] - cumulative)
    dx_outer = to_end[:, :, None] * jnp.einsum('hpn,sn->shp', grad_after, b_block.astype(jnp.float32), precision=highest)
    grad_b = grad_b + jnp.einsum('shp,hpn->sn', to_end[:, :, None] * x_heads, grad_after, precision=highest)
    grad_c = grad_c + jnp.einsum('shp,hpn->sn', jnp.exp(cumulative)[:, :, None] * d_heads, state_before, precision=highest)
    return (dx_inner + dx_outer).reshape(S, DI), grad_b, grad_c


def frame_attention(query_rows, key_rows, value_rows, dout_rows):
    head_count = DI // ATTENTION_WIDTH
    score_scale = ATTENTION_WIDTH ** -0.5
    query_h = query_rows.astype(jnp.float32).reshape(S, head_count, ATTENTION_WIDTH)
    key_h = key_rows.astype(jnp.float32).reshape(3 * S, head_count, ATTENTION_WIDTH)
    value_h = value_rows.astype(jnp.float32).reshape(3 * S, head_count, ATTENTION_WIDTH)
    dout_h = dout_rows.astype(jnp.float32).reshape(S, head_count, ATTENTION_WIDTH)
    scores = jnp.einsum('qhd,khd->hqk', query_h, key_h) * score_scale
    maxima = jnp.max(scores, axis=-1)
    log_norm = maxima + jnp.log(jnp.sum(jnp.exp(scores - maxima[..., None]), axis=-1))
    attn_probs = jnp.exp(scores - log_norm[..., None])
    probs_b = lax.optimization_barrier(attn_probs.astype(jnp.bfloat16)).astype(jnp.float32)
    attn_out = jnp.einsum('hqk,khd->qhd', probs_b, value_h)
    deltas = jnp.sum(dout_h * attn_out, axis=-1).T
    dprobs = jnp.einsum('qhd,khd->hqk', dout_h, value_h)
    dscores = attn_probs * (dprobs - deltas[..., None])
    dscore_b = lax.optimization_barrier(dscores.astype(jnp.bfloat16)).astype(jnp.float32)
    grad_q = jnp.einsum('hqk,khd->qhd', dscore_b, key_h) * score_scale
    key_summands = jnp.einsum('hqk,qhd->khd', dscore_b, query_h) * score_scale
    content_summands = jnp.einsum('hqk,qhd->khd', probs_b, dout_h)
    return grad_q.reshape(S, DI), key_summands.reshape(3 * S, DI), content_summands.reshape(3 * S, DI)


def reference(mixer_input, state_input, state_output, log_decay, queries, attn_keys, out_grad, frame_offsets, sink_frame_index):
    head_count = DI // HEADDIM
    x_blocks = mixer_input.reshape(NF, S, DI)
    b_blocks = state_input.reshape(NF, S, NSTATE)
    c_blocks = state_output.reshape(NF, S, NSTATE)
    decay_blocks = log_decay.reshape(NF, S, head_count)
    dout_blocks = out_grad.reshape(NF, S, DI)
    query_blocks = queries.reshape(NF, S, DI)
    key_blocks = attn_keys.reshape(NF, S, DI)
    state_parts, grad_parts, endings = lax.map(lambda group_args: block_parts(*group_args), (x_blocks, b_blocks, c_blocks, decay_blocks, dout_blocks))
    zero_state = jnp.zeros((head_count, HEADDIM, NSTATE), jnp.float32)

    def forward_step(carried, scan_item):
        local_part, ending = scan_item
        return jnp.exp(ending)[:, None, None] * carried + local_part, carried

    def reverse_step(carried, scan_item):
        local_part, ending = scan_item
        return local_part + jnp.exp(ending)[:, None, None] * carried, carried

    _, befores = lax.scan(forward_step, zero_state, (state_parts, endings))
    _, afters = lax.scan(reverse_step, zero_state, (grad_parts, endings), reverse=True)
    ssm_grad, grad_b, grad_c = lax.map(lambda group_args: block_grads(*group_args), (x_blocks, b_blocks, c_blocks, decay_blocks, dout_blocks, befores, afters))
    sink_index = sink_frame_index[0]

    def frame_step(carried, frame_index):
        acc_keys, accumulated_values = carried
        other_frame = jnp.maximum(frame_index - frame_offsets[frame_index], 0)
        key_rows = jnp.concatenate([key_blocks[frame_index], key_blocks[other_frame], key_blocks[sink_index]], axis=0)
        value_rows = jnp.concatenate([x_blocks[frame_index], x_blocks[other_frame], x_blocks[sink_index]], axis=0)
        grad_q, key_summands, content_summands = frame_attention(query_blocks[frame_index], key_rows, value_rows, dout_blocks[frame_index])
        acc_keys = acc_keys.at[frame_index].add(key_summands[:S])
        acc_keys = acc_keys.at[other_frame].add(key_summands[S:2 * S])
        acc_keys = acc_keys.at[sink_index].add(key_summands[2 * S:])
        accumulated_values = accumulated_values.at[frame_index].add(content_summands[:S])
        accumulated_values = accumulated_values.at[other_frame].add(content_summands[S:2 * S])
        accumulated_values = accumulated_values.at[sink_index].add(content_summands[2 * S:])
        return (acc_keys, accumulated_values), grad_q

    empty = jnp.zeros((NF, S, DI), jnp.float32)
    (acc_keys, accumulated_values), grad_q = lax.scan(frame_step, (empty, empty), jnp.arange(NF, dtype=jnp.int32))
    grad_input = (ssm_grad + accumulated_values).reshape(VIDEO_SPAN_ITEMS, DI).astype(jnp.bfloat16)
    grad_queries = grad_q.reshape(VIDEO_SPAN_ITEMS, DI).astype(jnp.bfloat16)
    grad_keys = acc_keys.reshape(VIDEO_SPAN_ITEMS, DI).astype(jnp.bfloat16)
    return grad_input, grad_queries, grad_keys, grad_b.reshape(VIDEO_SPAN_ITEMS, NSTATE), grad_c.reshape(VIDEO_SPAN_ITEMS, NSTATE)
```

```python
import jax
import jax.numpy as jnp
from jax import lax
from jax.experimental import pallas as pl
from jax.experimental.pallas import tpu as pltpu
from jax.sharding import PartitionSpec as P

DI = 2048
HEADDIM = 64
NSTATE = 128
ATTENTION_WIDTH = 128
S = 128
FR_DEV = 2
OFFMAX = 2
HEADS = DI // HEADDIM
GROUPS = DI // 128
ROWS = FR_DEV * S
F32 = jnp.float32
BF16 = jnp.bfloat16


def mm(a, b):
    return lax.dot_general(a, b, (((1,), (0,)), ((), ())), preferred_element_type=F32)


def mm_nt(a, b):
    return lax.dot_general(a, b, (((1,), (1,)), ((), ())), preferred_element_type=F32)


def mm_tn(a, b):
    return lax.dot_general(a, b, (((0,), (0,)), ((), ())), preferred_element_type=F32)


def decay_terms(cum_ref):
    rows = cum_ref[0]
    cols = jnp.transpose(rows)
    lane = lax.broadcasted_iota(jnp.int32, (S, 128), 1) < HEADDIM
    sub = lax.broadcasted_iota(jnp.int32, (128, NSTATE), 0) < HEADDIM
    blocks = []
    for b in range(FR_DEV):
        span = slice(b * S, (b + 1) * S)
        row = [rows[j : j + 1, span] for j in range(2)]
        col = [cols[span, j : j + 1] for j in range(2)]
        end = [r[:, S - 1 : S] for r in row]
        to_end = jnp.where(lane, jnp.exp(end[0] - col[0]), jnp.exp(end[1] - col[1]))
        grown = jnp.where(lane, jnp.exp(col[0]), jnp.exp(col[1]))
        whole = jnp.where(sub, jnp.exp(end[0]), jnp.exp(end[1]))
        blocks.append((row, col, to_end, grown, whole))
    return lane, blocks


def local_kernel(
    cum_ref, x_ref, g_ref, b_ref, c_ref,
    dx_ref, sp_ref, gp_ref, ls_ref, lg_ref, gb_ref, gc_ref,
    cb_ref, fold_ref,
):
    step = pl.program_id(0)

    @pl.when(step == 0)
    def _():
        for b in range(FR_DEV):
            span = slice(b * S, (b + 1) * S)
            cb_ref[b] = mm_nt(b_ref[span, :], c_ref[span, :])
            fold_ref[b] = jnp.zeros((S, S), F32)

    lane, blocks = decay_terms(cum_ref)
    causal = lax.broadcasted_iota(jnp.int32, (S, S), 0) <= lax.broadcasted_iota(
        jnp.int32, (S, S), 1
    )
    states, grads = [], []
    for b in range(FR_DEV):
        span = slice(b * S, (b + 1) * S)
        row, col, to_end, grown, whole = blocks[b]
        x = x_ref[span, :]
        g = g_ref[span, :]
        xf = x.astype(F32)
        inner, folded = [], None
        for j in range(2):
            weights = jnp.exp(jnp.where(causal, row[j] - col[j], -1e30))
            mixing = (weights * cb_ref[b]).astype(BF16)
            x_head = jnp.where(lane if j == 0 else ~lane, xf, 0.0).astype(BF16)
            term = weights * mm_nt(x_head, g)
            folded = term if folded is None else folded + term
            inner.append(mm(mixing, g))
        fold_ref[b] += folded
        dx_ref[span, :] = jnp.where(lane, inner[0], inner[1])
        x_scaled = (xf * to_end).astype(BF16)
        g_scaled = (g.astype(F32) * grown).astype(BF16)
        states.append(mm_tn(x_scaled, b_ref[span, :]))
        grads.append(mm_tn(g_scaled, c_ref[span, :]))
    sp_ref[...] = states[0]
    gp_ref[...] = grads[1]
    ls_ref[...] = (blocks[1][4] * states[0] + states[1]).astype(BF16)
    lg_ref[...] = (grads[0] + blocks[0][4] * grads[1]).astype(BF16)

    @pl.when(step == GROUPS - 1)
    def _():
        for b in range(FR_DEV):
            span = slice(b * S, (b + 1) * S)
            folded_b = fold_ref[b].astype(BF16)
            gb_ref[span, :] = mm(folded_b, c_ref[span, :])
            gc_ref[span, :] = mm_tn(folded_b, b_ref[span, :])


def scan_kernel(heads, rows, in_ref, out_ref):
    count = in_ref.shape[0]
    decays = []
    for d in range(count):
        tail = in_ref[d, 2 * rows :, :].astype(F32)
        decays.append(tail)
    for j in range(heads):
        for back in range(2):
            lo = back * rows + j * HEADDIM
            carry = jnp.zeros((HEADDIM, NSTATE), F32)
            for turn in range(count):
                d = count - 1 - turn if back else turn
                out_ref[d, lo : lo + HEADDIM, :] = carry.astype(BF16)
                decay = (
                    decays[d][3 * j : 3 * j + 1, :]
                    + decays[d][3 * j + 1 : 3 * j + 2, :]
                    + decays[d][3 * j + 2 : 3 * j + 3, :]
                )
                carry = decay * carry + in_ref[d, lo : lo + HEADDIM, :].astype(F32)


def attn_kernel(
    t_ref, q_ref, k_ref, x_ref, g_ref, pk_ref, pv_ref, sk_ref, sv_ref,
    gq_ref, ok_ref, ov_ref, rk_ref, rv_ref, sink_ref,
    kp_ref, vp_ref,
):
    scale = ATTENTION_WIDTH ** (-0.5)
    for pool, behind, own in ((kp_ref, pk_ref, k_ref), (vp_ref, pv_ref, x_ref)):
        pool[0:ROWS, :] = behind[...]
        pool[ROWS : 2 * ROWS, :] = own[...]
    parts = []
    for i in range(FR_DEV):
        span = slice(i * S, (i + 1) * S)
        other = pl.ds(pl.multiple_of(t_ref[i] * S, S), S)
        q = q_ref[span, :]
        g = g_ref[span, :]
        keys = jnp.concatenate([k_ref[span, :], kp_ref[other, :], sk_ref[...]], axis=0)
        values = jnp.concatenate([x_ref[span, :], vp_ref[other, :], sv_ref[...]], axis=0)
        scores = mm_nt(q, keys) * scale
        powers = jnp.exp(scores - jnp.max(scores, axis=1, keepdims=True))
        probs = powers * (1.0 / jnp.sum(powers, axis=1, keepdims=True))
        probs_b = probs.astype(BF16)
        out = mm(probs_b, values)
        delta = jnp.sum(g.astype(F32) * out, axis=1, keepdims=True)
        dscores = (probs * (mm_nt(g, values) - delta)).astype(BF16)
        gq_ref[span, :] = (mm(dscores, keys) * scale).astype(BF16)
        parts.append((mm_tn(dscores, q) * scale, mm_tn(probs_b, g)))
    hits = [[(t_ref[i] == j).astype(F32) for j in range(2 * FR_DEV)] for i in range(FR_DEV)]
    for c, (own_ref, back_ref) in enumerate(((ok_ref, rk_ref), (ov_ref, rv_ref))):
        others = [parts[i][c][S : 2 * S] for i in range(FR_DEV)]
        for j in range(FR_DEV):
            span = slice(j * S, (j + 1) * S)
            back_ref[span, :] = (hits[0][j] * others[0] + hits[1][j] * others[1]).astype(BF16)
            own_ref[span, :] = (
                parts[j][c][:S]
                + hits[0][FR_DEV + j] * others[0]
                + hits[1][FR_DEV + j] * others[1]
            )
        sink_ref[c * S : (c + 1) * S, :] = parts[0][c][2 * S :] + parts[1][c][2 * S :]


def final_kernel(
    own_ref, cum_ref, x_ref, g_ref, b_ref, c_ref, dx_ref, sp_ref, gp_ref, si_ref, gi_ref,
    gbl_ref, gcl_ref, ok_ref, ov_ref, rk_ref, rv_ref, sk_ref, sv_ref,
    gin_ref, gk_ref, gb_ref, gc_ref,
):
    @pl.when(pl.program_id(0) == 0)
    def _():
        gb_ref[...] = gbl_ref[...]
        gc_ref[...] = gcl_ref[...]

    _, blocks = decay_terms(cum_ref)
    state_in = si_ref[...].astype(F32)
    grad_in = gi_ref[...].astype(F32)
    befores = [state_in, blocks[0][4] * state_in + sp_ref[...]]
    afters = [gp_ref[...] + blocks[1][4] * grad_in, grad_in]
    for b in range(FR_DEV):
        span = slice(b * S, (b + 1) * S)
        _, _, to_end, grown, _ = blocks[b]
        mine = (own_ref[0] == b).astype(F32)
        after = afters[b].astype(BF16)
        before = befores[b].astype(BF16)
        x_scaled = (x_ref[span, :].astype(F32) * to_end).astype(BF16)
        g_scaled = (g_ref[span, :].astype(F32) * grown).astype(BF16)
        outer = to_end * mm_nt(b_ref[span, :], after)
        gb_ref[span, :] += mm(x_scaled, after)
        gc_ref[span, :] += mm(g_scaled, before)
        gin_ref[span, :] = (
            dx_ref[span, :]
            + outer
            + ov_ref[span, :]
            + rv_ref[span, :].astype(F32)
            + mine * sv_ref[...].astype(F32)
        ).astype(BF16)
        gk_ref[span, :] = (
            ok_ref[span, :] + rk_ref[span, :].astype(F32) + mine * sk_ref[...].astype(F32)
        ).astype(BF16)


def swap(value, axis, bit):
    return lax.ppermute(value, axis, [(i, i ^ bit) for i in range(lax.axis_size(axis))])


def halve(value, axis):
    place = lax.axis_index(axis)
    bit = 1
    while bit < lax.axis_size(axis):
        high = (place // bit) % 2
        half = value.shape[0] // 2
        keep = lax.dynamic_slice_in_dim(value, high * half, half)
        give = lax.dynamic_slice_in_dim(value, (1 - high) * half, half)
        value = keep + swap(give.astype(BF16), axis, bit).astype(value.dtype)
        bit *= 2
    return value


def double(value, axis):
    place = lax.axis_index(axis)
    bit = lax.axis_size(axis) // 2
    while bit:
        high = (place // bit) % 2 == 1
        got = swap(value, axis, bit)
        value = jnp.concatenate([jnp.where(high, got, value), jnp.where(high, value, got)])
        bit //= 2
    return value


def shift(value, axis, by):
    peers = lax.axis_size(axis)
    return lax.ppermute(
        value, axis, [(i, i + by) for i in range(peers) if 0 <= i + by < peers]
    )


def shards(
    mixer_input, state_input, state_output, log_decay, queries, attn_keys, out_grad,
    frame_offsets, sink_frame_index,
):
    peers = lax.axis_size("frame")
    device = lax.axis_index("frame")
    first_frame = device * FR_DEV
    params = pltpu.CompilerParams(vmem_limit_bytes=40 * 1024 * 1024)

    cols = pl.BlockSpec((ROWS, 128), lambda a, *_: (0, a))
    frame_lo = pl.BlockSpec((S, 128), lambda a, *_: (0, a))
    frame_hi = pl.BlockSpec((S, 128), lambda a, *_: (1, a))
    state = pl.BlockSpec((128, NSTATE), lambda a, *_: (a, 0))
    fixed = pl.BlockSpec((ROWS, NSTATE), lambda a, *_: (0, 0))
    cum_spec = pl.BlockSpec((1, 8, ROWS), lambda a, *_: (a, 0, 0))
    wide = lambda dtype: jax.ShapeDtypeStruct((ROWS, DI), dtype)
    tall = lambda dtype: jax.ShapeDtypeStruct((DI, NSTATE), dtype)
    small = jax.ShapeDtypeStruct((ROWS, NSTATE), F32)

    behind_k = shift(attn_keys, "frame", 1)
    behind_v = shift(mixer_input, "frame", 1)
    sink_index = sink_frame_index[0]
    sink_owner = sink_index // FR_DEV
    sink_slot = sink_index % FR_DEV
    picked = jnp.concatenate(
        [
            lax.dynamic_slice_in_dim(attn_keys, sink_slot * S, S),
            lax.dynamic_slice_in_dim(mixer_input, sink_slot * S, S),
        ]
    )
    picked = jnp.where(device == sink_owner, picked, jnp.zeros_like(picked))
    sink_pair = double(halve(picked, "frame"), "frame")

    before = jnp.triu(jnp.ones((S, S), F32))
    cumulative = jnp.einsum(
        "bsh,st->hbt",
        log_decay.reshape(FR_DEV, S, HEADS),
        before,
        precision=lax.Precision.HIGHEST,
    )
    total = jnp.exp(jnp.sum(cumulative[:, :, -1], axis=1))
    cum_rows = cumulative.reshape(GROUPS, 2, ROWS)
    cum_rows = jnp.pad(cum_rows, ((0, 0), (0, 6), (0, 0)))
    dx, sp, gp, local_state, local_grad, gb_local, gc_local = pl.pallas_call(
        local_kernel,
        grid=(GROUPS,),
        in_specs=[cum_spec, cols, cols, fixed, fixed],
        out_specs=[cols, state, state, state, state, fixed, fixed],
        out_shape=[wide(F32), tall(F32), tall(F32), tall(BF16), tall(BF16), small, small],
        scratch_shapes=[pltpu.VMEM((FR_DEV, S, S), F32), pltpu.VMEM((FR_DEV, S, S), F32)],
        compiler_params=params,
        cost_estimate=pl.CostEstimate(
            flops=1_000_000_000, bytes_accessed=10_000_000, transcendentals=1_500_000
        ),
    )(cum_rows, mixer_input, out_grad, state_input, state_output)

    heads = HEADS // peers
    rows = DI // peers
    high = total.astype(BF16)
    rest = total - high.astype(F32)
    mid = rest.astype(BF16)
    low = (rest - mid.astype(F32)).astype(BF16)
    decay_rows = jnp.stack([high, mid, low], axis=-1).reshape(peers, heads * 3, 1)
    decay_rows = jnp.pad(decay_rows, ((0, 0), (0, 16 - heads * 3), (0, 0)))
    decay_rows = jnp.broadcast_to(decay_rows, (peers, 16, NSTATE))
    sent = jnp.concatenate(
        [
            local_state.reshape(peers, rows, NSTATE),
            local_grad.reshape(peers, rows, NSTATE),
            decay_rows,
        ],
        axis=1,
    )
    got = lax.all_to_all(sent, "frame", 0, 0)
    scanned = pl.pallas_call(
        lambda *refs: scan_kernel(heads, rows, *refs),
        out_shape=jax.ShapeDtypeStruct((peers, 2 * rows, NSTATE), BF16),
        compiler_params=params,
    )(got)
    entered = lax.all_to_all(scanned, "frame", 0, 0)
    state_in = entered[:, :rows].reshape(DI, NSTATE)
    grad_in = entered[:, rows:].reshape(DI, NSTATE)

    frame_ids = first_frame + jnp.arange(FR_DEV, dtype=jnp.int32)
    own_offsets = lax.dynamic_slice_in_dim(frame_offsets, first_frame, FR_DEV)
    target = jnp.maximum(frame_ids - own_offsets, 0) - first_frame + OFFMAX
    grad_q, own_k, own_v, back_k, back_v, sink_terms = pl.pallas_call(
        attn_kernel,
        grid_spec=pltpu.PrefetchScalarGridSpec(
            num_scalar_prefetch=1,
            grid=(GROUPS,),
            in_specs=[cols] * 6 + [frame_lo, frame_hi],
            out_specs=[cols] * 6,
            scratch_shapes=[pltpu.VMEM((2 * ROWS, 128), BF16), pltpu.VMEM((2 * ROWS, 128), BF16)],
        ),
        out_shape=[wide(BF16), wide(F32), wide(F32), wide(BF16), wide(BF16), wide(F32)],
        compiler_params=params,
        cost_estimate=pl.CostEstimate(
            flops=3_000_000_000, bytes_accessed=14_000_000, transcendentals=1_600_000
        ),
    )(target, queries, attn_keys, mixer_input, out_grad, behind_k, behind_v, sink_pair, sink_pair)

    returned_k = shift(back_k, "frame", -1)
    returned_v = shift(back_v, "frame", -1)
    sink_grads = double(halve(sink_terms, "frame").astype(BF16), "frame")
    owned = jnp.where(device == sink_owner, sink_slot, -1).astype(jnp.int32).reshape(1)

    grad_input, grad_keys, grad_b, grad_c = pl.pallas_call(
        final_kernel,
        grid_spec=pltpu.PrefetchScalarGridSpec(
            num_scalar_prefetch=1,
            grid=(GROUPS,),
            in_specs=[cum_spec, cols, cols, fixed, fixed, cols, state, state, state, state]
            + [fixed, fixed, cols, cols, cols, cols, frame_lo, frame_hi],
            out_specs=[cols, cols, fixed, fixed],
        ),
        out_shape=[wide(BF16), wide(BF16), small, small],
        compiler_params=params,
    )(
        owned, cum_rows, mixer_input, out_grad, state_input, state_output, dx, sp, gp,
        state_in, grad_in, gb_local, gc_local, own_k, own_v, returned_k, returned_v,
        sink_grads, sink_grads,
    )
    return (grad_input, grad_q, grad_keys, grad_b, grad_c)


def solution(mesh):
    rows = P(("grp", "frame"), None)
    return jax.shard_map(
        shards,
        mesh=mesh,
        in_specs=(rows,) * 7 + (P("grp"), P("grp")),
        out_specs=(rows,) * 5,
        check_vma=False,
    )
```

```python
import jax
import jax.numpy as jnp
from jax import lax
from jax.experimental import pallas as pl
from jax.experimental.pallas import tpu as pltpu
from jax.sharding import PartitionSpec as P

DI = 2048
HEADDIM = 64
NSTATE = 128
ATTENTION_WIDTH = 128
S = 128
FR_DEV = 2
OFFMAX = 2
HEADS = DI // HEADDIM
GROUPS = DI // 128
ROWS = FR_DEV * S
F32 = jnp.float32
BF16 = jnp.bfloat16


def mm(a, b):
    return lax.dot_general(a, b, (((1,), (0,)), ((), ())), preferred_element_type=F32)


def mm_nt(a, b):
    return lax.dot_general(a, b, (((1,), (1,)), ((), ())), preferred_element_type=F32)


def mm_tn(a, b):
    return lax.dot_general(a, b, (((0,), (0,)), ((), ())), preferred_element_type=F32)


def decay_terms(cum_ref):
    rows = cum_ref[0]
    cols = jnp.transpose(rows)
    lane = lax.broadcasted_iota(jnp.int32, (S, 128), 1) < HEADDIM
    sub = lax.broadcasted_iota(jnp.int32, (128, NSTATE), 0) < HEADDIM
    blocks = []
    for b in range(FR_DEV):
        span = slice(b * S, (b + 1) * S)
        row = [rows[j : j + 1, span] for j in range(2)]
        col = [cols[span, j : j + 1] for j in range(2)]
        end = [r[:, S - 1 : S] for r in row]
        to_end = jnp.where(lane, jnp.exp(end[0] - col[0]), jnp.exp(end[1] - col[1]))
        grown = jnp.where(lane, jnp.exp(col[0]), jnp.exp(col[1]))
        whole = jnp.where(sub, jnp.exp(end[0]), jnp.exp(end[1]))
        blocks.append((row, col, to_end, grown, whole))
    return lane, blocks


def local_kernel(
    cum_ref, x_ref, g_ref, b_ref, c_ref,
    dx_ref, sp_ref, gp_ref, ls_ref, lg_ref, gb_ref, gc_ref,
    cb_ref, fold_ref,
):
    step = pl.program_id(0)

    @pl.when(step == 0)
    def _():
        for b in range(FR_DEV):
            span = slice(b * S, (b + 1) * S)
            cb_ref[b] = mm_nt(b_ref[span, :], c_ref[span, :])
            fold_ref[b] = jnp.zeros((S, S), F32)

    lane, blocks = decay_terms(cum_ref)
    causal = lax.broadcasted_iota(jnp.int32, (S, S), 0) <= lax.broadcasted_iota(
        jnp.int32, (S, S), 1
    )
    states, grads = [], []
    for b in range(FR_DEV):
        span = slice(b * S, (b + 1) * S)
        row, col, to_end, grown, whole = blocks[b]
        x = x_ref[span, :]
        g = g_ref[span, :]
        xf = x.astype(F32)
        inner, folded = [], None
        for j in range(2):
            weights = jnp.exp(jnp.where(causal, row[j] - col[j], -1e30))
            mixing = (weights * cb_ref[b]).astype(BF16)
            x_head = jnp.where(lane if j == 0 else ~lane, xf, 0.0).astype(BF16)
            term = weights * mm_nt(x_head, g)
            folded = term if folded is None else folded + term
            inner.append(mm(mixing, g))
        fold_ref[b] += folded
        dx_ref[span, :] = jnp.where(lane, inner[0], inner[1])
        x_scaled = (xf * to_end).astype(BF16)
        g_scaled = (g.astype(F32) * grown).astype(BF16)
        states.append(mm_tn(x_scaled, b_ref[span, :]))
        grads.append(mm_tn(g_scaled, c_ref[span, :]))
    sp_ref[...] = states[0]
    gp_ref[...] = grads[1]
    ls_ref[...] = (blocks[1][4] * states[0] + states[1]).astype(BF16)
    lg_ref[...] = (grads[0] + blocks[0][4] * grads[1]).astype(BF16)

    @pl.when(step == GROUPS - 1)
    def _():
        for b in range(FR_DEV):
            span = slice(b * S, (b + 1) * S)
            folded_b = fold_ref[b].astype(BF16)
            gb_ref[span, :] = mm(folded_b, c_ref[span, :])
            gc_ref[span, :] = mm_tn(folded_b, b_ref[span, :])


def scan_kernel(heads, rows, in_ref, out_ref):
    count = in_ref.shape[0]
    decays = []
    for d in range(count):
        tail = in_ref[d, 2 * rows :, :].astype(F32)
        decays.append(tail)
    for j in range(heads):
        for back in range(2):
            lo = back * rows + j * HEADDIM
            carry = jnp.zeros((HEADDIM, NSTATE), F32)
            for turn in range(count):
                d = count - 1 - turn if back else turn
                out_ref[d, lo : lo + HEADDIM, :] = carry.astype(BF16)
                decay = (
                    decays[d][3 * j : 3 * j + 1, :]
                    + decays[d][3 * j + 1 : 3 * j + 2, :]
                    + decays[d][3 * j + 2 : 3 * j + 3, :]
                )
                carry = decay * carry + in_ref[d, lo : lo + HEADDIM, :].astype(F32)


def attn_kernel(
    t_ref, q_ref, k_ref, x_ref, g_ref, pk0_ref, pk1_ref, pv0_ref, pv1_ref, sk_ref, sv_ref,
    gq_ref, ok_ref, ov_ref, rk_ref, rv_ref, sink_ref,
    kp_ref, vp_ref,
):
    scale = ATTENTION_WIDTH ** (-0.5)
    for pool, first, second, own in (
        (kp_ref, pk0_ref, pk1_ref, k_ref),
        (vp_ref, pv0_ref, pv1_ref, x_ref),
    ):
        pool[0:S, :] = first[...]
        pool[S:ROWS, :] = second[...]
        pool[ROWS : 2 * ROWS, :] = own[...]
    parts = []
    for i in range(FR_DEV):
        span = slice(i * S, (i + 1) * S)
        other = pl.ds(pl.multiple_of(t_ref[i] * S, S), S)
        q = q_ref[span, :]
        g = g_ref[span, :]
        keys = jnp.concatenate([k_ref[span, :], kp_ref[other, :], sk_ref[...]], axis=0)
        values = jnp.concatenate([x_ref[span, :], vp_ref[other, :], sv_ref[...]], axis=0)
        scores = mm_nt(q, keys) * scale
        powers = jnp.exp(scores - jnp.max(scores, axis=1, keepdims=True))
        probs = powers * (1.0 / jnp.sum(powers, axis=1, keepdims=True))
        probs_b = probs.astype(BF16)
        out = mm(probs_b, values)
        delta = jnp.sum(g.astype(F32) * out, axis=1, keepdims=True)
        dscores = (probs * (mm_nt(g, values) - delta)).astype(BF16)
        gq_ref[span, :] = (mm(dscores, keys) * scale).astype(BF16)
        parts.append((mm_tn(dscores, q) * scale, mm_tn(probs_b, g)))
    hits = [[(t_ref[i] == j).astype(F32) for j in range(2 * FR_DEV)] for i in range(FR_DEV)]
    for c, (own_ref, back_ref) in enumerate(((ok_ref, rk_ref), (ov_ref, rv_ref))):
        others = [parts[i][c][S : 2 * S] for i in range(FR_DEV)]
        for j in range(FR_DEV):
            span = slice(j * S, (j + 1) * S)
            back_ref[span, :] = (hits[0][j] * others[0] + hits[1][j] * others[1]).astype(BF16)
            own_ref[span, :] = (
                parts[j][c][:S]
                + hits[0][FR_DEV + j] * others[0]
                + hits[1][FR_DEV + j] * others[1]
            )
        sink_ref[c * S : (c + 1) * S, :] = parts[0][c][2 * S :] + parts[1][c][2 * S :]


def final_kernel(
    own_ref, cum_ref, x_ref, g_ref, b_ref, c_ref, dx_ref, sp_ref, gp_ref, si_ref, gi_ref,
    gbl_ref, gcl_ref, ok_ref, ov_ref, rk0_ref, rk1_ref, rv0_ref, rv1_ref, sk_ref, sv_ref,
    gin_ref, gk_ref, gb_ref, gc_ref,
):
    @pl.when(pl.program_id(0) == 0)
    def _():
        gb_ref[...] = gbl_ref[...]
        gc_ref[...] = gcl_ref[...]

    _, blocks = decay_terms(cum_ref)
    state_in = si_ref[...].astype(F32)
    grad_in = gi_ref[...].astype(F32)
    befores = [state_in, blocks[0][4] * state_in + sp_ref[...]]
    afters = [gp_ref[...] + blocks[1][4] * grad_in, grad_in]
    for b in range(FR_DEV):
        span = slice(b * S, (b + 1) * S)
        _, _, to_end, grown, _ = blocks[b]
        mine = (own_ref[0] == b).astype(F32)
        after = afters[b].astype(BF16)
        before = befores[b].astype(BF16)
        x_scaled = (x_ref[span, :].astype(F32) * to_end).astype(BF16)
        g_scaled = (g_ref[span, :].astype(F32) * grown).astype(BF16)
        outer = to_end * mm_nt(b_ref[span, :], after)
        gb_ref[span, :] += mm(x_scaled, after)
        gc_ref[span, :] += mm(g_scaled, before)
        gin_ref[span, :] = (
            dx_ref[span, :]
            + outer
            + ov_ref[span, :]
            + (rv0_ref, rv1_ref)[b][...].astype(F32)
            + mine * sv_ref[...].astype(F32)
        ).astype(BF16)
        gk_ref[span, :] = (
            ok_ref[span, :] + (rk0_ref, rk1_ref)[b][...].astype(F32) + mine * sk_ref[...].astype(F32)
        ).astype(BF16)


def swap(value, axis, bit):
    return lax.ppermute(value, axis, [(i, i ^ bit) for i in range(lax.axis_size(axis))])


def beside(value, waiting, done):
    if not waiting:
        return value
    value, arrived = lax.optimization_barrier((value, waiting.pop(0)))
    done.append(arrived)
    return value


def halve(value, axis, bit, stop, waiting=(), done=()):
    place = lax.axis_index(axis)
    while bit < stop:
        high = (place // bit) % 2
        half = value.shape[0] // 2
        keep = lax.dynamic_slice_in_dim(value, high * half, half)
        give = lax.dynamic_slice_in_dim(value, (1 - high) * half, half)
        value = keep + swap(give.astype(BF16), axis, bit).astype(value.dtype)
        value = beside(value, waiting, done)
        bit *= 2
    return value


def double(value, axis, waiting=(), done=()):
    place = lax.axis_index(axis)
    bit = lax.axis_size(axis) // 2
    while bit:
        high = (place // bit) % 2 == 1
        got = swap(value, axis, bit)
        value = jnp.concatenate([jnp.where(high, got, value), jnp.where(high, value, got)])
        value = beside(value, waiting, done)
        bit //= 2
    return value


def shift(value, axis, by):
    peers = lax.axis_size(axis)
    return lax.ppermute(
        value, axis, [(i, i + by) for i in range(peers) if 0 <= i + by < peers]
    )


def shards(
    mixer_input, state_input, state_output, log_decay, queries, attn_keys, out_grad,
    frame_offsets, sink_frame_index,
):
    peers = lax.axis_size("frame")
    device = lax.axis_index("frame")
    first_frame = device * FR_DEV
    params = pltpu.CompilerParams(vmem_limit_bytes=40 * 1024 * 1024)

    cols = pl.BlockSpec((ROWS, 128), lambda a, *_: (0, a))
    frame_lo = pl.BlockSpec((S, 128), lambda a, *_: (0, a))
    frame_hi = pl.BlockSpec((S, 128), lambda a, *_: (1, a))
    state = pl.BlockSpec((128, NSTATE), lambda a, *_: (a, 0))
    fixed = pl.BlockSpec((ROWS, NSTATE), lambda a, *_: (0, 0))
    cum_spec = pl.BlockSpec((1, 8, ROWS), lambda a, *_: (a, 0, 0))
    wide = lambda dtype: jax.ShapeDtypeStruct((ROWS, DI), dtype)
    tall = lambda dtype: jax.ShapeDtypeStruct((DI, NSTATE), dtype)
    small = jax.ShapeDtypeStruct((ROWS, NSTATE), F32)

    behind = [
        shift(a[i * S : (i + 1) * S], "frame", 1)
        for a in (attn_keys, mixer_input)
        for i in range(FR_DEV)
    ]
    sink_index = sink_frame_index[0]
    sink_owner = sink_index // FR_DEV
    sink_slot = sink_index % FR_DEV
    picked = jnp.concatenate(
        [
            lax.dynamic_slice_in_dim(attn_keys, sink_slot * S, S),
            lax.dynamic_slice_in_dim(mixer_input, sink_slot * S, S),
        ]
    )
    picked = jnp.where(device == sink_owner, picked, jnp.zeros_like(picked))
    sink_part = halve(picked, "frame", 1, 2)

    before = jnp.triu(jnp.ones((S, S), F32))
    cumulative = jnp.einsum(
        "bsh,st->hbt",
        log_decay.reshape(FR_DEV, S, HEADS),
        before,
        precision=lax.Precision.HIGHEST,
    )
    total = jnp.exp(jnp.sum(cumulative[:, :, -1], axis=1))
    cum_rows = cumulative.reshape(GROUPS, 2, ROWS)
    cum_rows = jnp.pad(cum_rows, ((0, 0), (0, 6), (0, 0)))
    dx, sp, gp, local_state, local_grad, gb_local, gc_local = pl.pallas_call(
        local_kernel,
        grid=(GROUPS,),
        in_specs=[cum_spec, cols, cols, fixed, fixed],
        out_specs=[cols, state, state, state, state, fixed, fixed],
        out_shape=[wide(F32), tall(F32), tall(F32), tall(BF16), tall(BF16), small, small],
        scratch_shapes=[pltpu.VMEM((FR_DEV, S, S), F32), pltpu.VMEM((FR_DEV, S, S), F32)],
        compiler_params=params,
        cost_estimate=pl.CostEstimate(
            flops=1_000_000_000, bytes_accessed=10_000_000, transcendentals=1_500_000
        ),
    )(cum_rows, mixer_input, out_grad, state_input, state_output)

    heads = HEADS // peers
    rows = DI // peers
    high = total.astype(BF16)
    rest = total - high.astype(F32)
    mid = rest.astype(BF16)
    low = (rest - mid.astype(F32)).astype(BF16)
    decay_rows = jnp.stack([high, mid, low], axis=-1).reshape(peers, heads * 3, 1)
    decay_rows = jnp.pad(decay_rows, ((0, 0), (0, 16 - heads * 3), (0, 0)))
    decay_rows = jnp.broadcast_to(decay_rows, (peers, 16, NSTATE))
    sent = jnp.concatenate(
        [
            local_state.reshape(peers, rows, NSTATE),
            local_grad.reshape(peers, rows, NSTATE),
            decay_rows,
        ],
        axis=1,
    )
    sink_part, sent, early = lax.optimization_barrier((sink_part, sent, behind[:2]))
    waiting = behind[2:] + [lax.all_to_all(sent, "frame", 0, 0)]
    done = []
    sink_part = halve(sink_part, "frame", 2, peers, waiting, done)
    sink_pair = double(sink_part, "frame", waiting, done)
    behind, got = list(early) + done[:2], done[2]
    scanned = pl.pallas_call(
        lambda *refs: scan_kernel(heads, rows, *refs),
        out_shape=jax.ShapeDtypeStruct((peers, 2 * rows, NSTATE), BF16),
        compiler_params=params,
    )(got)
    scanned, sink_pair = lax.optimization_barrier((scanned, sink_pair))
    entered = lax.all_to_all(scanned, "frame", 0, 0)

    frame_ids = first_frame + jnp.arange(FR_DEV, dtype=jnp.int32)
    own_offsets = lax.dynamic_slice_in_dim(frame_offsets, first_frame, FR_DEV)
    target = jnp.maximum(frame_ids - own_offsets, 0) - first_frame + OFFMAX
    grad_q, own_k, own_v, back_k, back_v, sink_terms = pl.pallas_call(
        attn_kernel,
        grid_spec=pltpu.PrefetchScalarGridSpec(
            num_scalar_prefetch=1,
            grid=(GROUPS,),
            in_specs=[cols] * 4 + [frame_lo] * 5 + [frame_hi],
            out_specs=[cols] * 6,
            scratch_shapes=[pltpu.VMEM((2 * ROWS, 128), BF16), pltpu.VMEM((2 * ROWS, 128), BF16)],
        ),
        out_shape=[wide(BF16), wide(F32), wide(F32), wide(BF16), wide(BF16), wide(F32)],
        compiler_params=params,
        cost_estimate=pl.CostEstimate(
            flops=3_000_000_000, bytes_accessed=14_000_000, transcendentals=1_600_000
        ),
    )(target, queries, attn_keys, mixer_input, out_grad, *behind, sink_pair, sink_pair)

    entered, sink_terms, back_k, back_v = lax.optimization_barrier(
        (entered, sink_terms, back_k, back_v)
    )
    state_in = entered[:, :rows].reshape(DI, NSTATE)
    grad_in = entered[:, rows:].reshape(DI, NSTATE)
    waiting = [
        shift(a[i * S : (i + 1) * S], "frame", -1)
        for a in (back_k, back_v)
        for i in range(FR_DEV)
    ]
    returned = []
    sink_part = halve(sink_terms, "frame", 1, 2)
    sink_part = halve(sink_part, "frame", 2, peers, waiting, returned)
    sink_grads = double(sink_part.astype(BF16), "frame", waiting, returned)
    owned = jnp.where(device == sink_owner, sink_slot, -1).astype(jnp.int32).reshape(1)

    grad_input, grad_keys, grad_b, grad_c = pl.pallas_call(
        final_kernel,
        grid_spec=pltpu.PrefetchScalarGridSpec(
            num_scalar_prefetch=1,
            grid=(GROUPS,),
            in_specs=[cum_spec, cols, cols, fixed, fixed, cols, state, state, state, state]
            + [fixed, fixed, cols, cols] + [frame_lo] * 5 + [frame_hi],
            out_specs=[cols, cols, fixed, fixed],
        ),
        out_shape=[wide(BF16), wide(BF16), small, small],
        compiler_params=params,
    )(
        owned, cum_rows, mixer_input, out_grad, state_input, state_output, dx, sp, gp,
        state_in, grad_in, gb_local, gc_local, own_k, own_v, *returned,
        sink_grads, sink_grads,
    )
    return (grad_input, grad_q, grad_keys, grad_b, grad_c)


def solution(mesh):
    rows = P(("grp", "frame"), None)
    return jax.shard_map(
        shards,
        mesh=mesh,
        in_specs=(rows,) * 7 + (P("grp"), P("grp")),
        out_specs=(rows,) * 5,
        check_vma=False,
    )
```

```python
import jax
import jax.numpy as jnp
from jax import lax
from jax.experimental import pallas as pl
from jax.experimental.pallas import tpu as pltpu
from jax.sharding import PartitionSpec as P

DI = 2048
HEADDIM = 64
NSTATE = 128
ATTENTION_WIDTH = 128
S = 128
FR_DEV = 2
OFFMAX = 2
HEADS = DI // HEADDIM
GROUPS = DI // 128
ROWS = FR_DEV * S
F32 = jnp.float32
BF16 = jnp.bfloat16


def mm(a, b):
    return lax.dot_general(a, b, (((1,), (0,)), ((), ())), preferred_element_type=F32)


def mm_nt(a, b):
    return lax.dot_general(a, b, (((1,), (1,)), ((), ())), preferred_element_type=F32)


def mm_tn(a, b):
    return lax.dot_general(a, b, (((0,), (0,)), ((), ())), preferred_element_type=F32)


def decay_terms(cum_ref):
    rows = cum_ref[0]
    cols = jnp.transpose(rows)
    lane = lax.broadcasted_iota(jnp.int32, (S, 128), 1) < HEADDIM
    sub = lax.broadcasted_iota(jnp.int32, (128, NSTATE), 0) < HEADDIM
    blocks = []
    for b in range(FR_DEV):
        span = slice(b * S, (b + 1) * S)
        row = [rows[j : j + 1, span] for j in range(2)]
        col = [cols[span, j : j + 1] for j in range(2)]
        end = [r[:, S - 1 : S] for r in row]
        to_end = jnp.where(lane, jnp.exp(end[0] - col[0]), jnp.exp(end[1] - col[1]))
        grown = jnp.where(lane, jnp.exp(col[0]), jnp.exp(col[1]))
        whole = jnp.where(sub, jnp.exp(end[0]), jnp.exp(end[1]))
        blocks.append((row, col, to_end, grown, whole))
    return lane, blocks


def local_kernel(
    cum_ref, x_ref, g_ref, b_ref, c_ref,
    dx_ref, sp_ref, gp_ref, ls_ref, lg_ref, gb_ref, gc_ref,
    cb_ref, fold_ref,
):
    step = pl.program_id(0)

    @pl.when(step == 0)
    def _():
        for b in range(FR_DEV):
            span = slice(b * S, (b + 1) * S)
            cb_ref[b] = mm_nt(b_ref[span, :], c_ref[span, :])
            fold_ref[b] = jnp.zeros((S, S), F32)

    lane, blocks = decay_terms(cum_ref)
    causal = lax.broadcasted_iota(jnp.int32, (S, S), 0) <= lax.broadcasted_iota(
        jnp.int32, (S, S), 1
    )
    states, grads = [], []
    for b in range(FR_DEV):
        span = slice(b * S, (b + 1) * S)
        row, col, to_end, grown, whole = blocks[b]
        x = x_ref[span, :]
        g = g_ref[span, :]
        xf = x.astype(F32)
        inner, folded = [], None
        for j in range(2):
            weights = jnp.exp(jnp.where(causal, row[j] - col[j], -1e30))
            mixing = (weights * cb_ref[b]).astype(BF16)
            x_head = jnp.where(lane if j == 0 else ~lane, xf, 0.0).astype(BF16)
            term = weights * mm_nt(x_head, g)
            folded = term if folded is None else folded + term
            inner.append(mm(mixing, g))
        fold_ref[b] += folded
        dx_ref[span, :] = jnp.where(lane, inner[0], inner[1])
        x_scaled = (xf * to_end).astype(BF16)
        g_scaled = (g.astype(F32) * grown).astype(BF16)
        states.append(mm_tn(x_scaled, b_ref[span, :]))
        grads.append(mm_tn(g_scaled, c_ref[span, :]))
    sp_ref[...] = states[0]
    gp_ref[...] = grads[1]
    ls_ref[...] = (blocks[1][4] * states[0] + states[1]).astype(BF16)
    lg_ref[...] = (grads[0] + blocks[0][4] * grads[1]).astype(BF16)

    @pl.when(step == GROUPS - 1)
    def _():
        for b in range(FR_DEV):
            span = slice(b * S, (b + 1) * S)
            folded_b = fold_ref[b].astype(BF16)
            gb_ref[span, :] = mm(folded_b, c_ref[span, :])
            gc_ref[span, :] = mm_tn(folded_b, b_ref[span, :])


def scan_kernel(heads, rows, in_ref, out_ref):
    count = in_ref.shape[0]
    decays = []
    for d in range(count):
        tail = in_ref[d, 2 * rows :, :].astype(F32)
        decays.append(tail)
    for j in range(heads):
        for back in range(2):
            lo = back * rows + j * HEADDIM
            carry = jnp.zeros((HEADDIM, NSTATE), F32)
            for turn in range(count):
                d = count - 1 - turn if back else turn
                out_ref[d, lo : lo + HEADDIM, :] = carry.astype(BF16)
                decay = (
                    decays[d][3 * j : 3 * j + 1, :]
                    + decays[d][3 * j + 1 : 3 * j + 2, :]
                    + decays[d][3 * j + 2 : 3 * j + 3, :]
                )
                carry = decay * carry + in_ref[d, lo : lo + HEADDIM, :].astype(F32)


def attn_kernel(
    t_ref, q_ref, k_ref, x_ref, g_ref, pk0_ref, pk1_ref, pv0_ref, pv1_ref, sk_ref, sv_ref,
    *refs,
):
    gq_ref, ok_ref, ov_ref, sink_ref, rk_ref, rv_ref, kp_ref, vp_ref = refs[-8:]
    scale = ATTENTION_WIDTH ** (-0.5)
    for pool, first, second, own in (
        (kp_ref, pk0_ref, pk1_ref, k_ref),
        (vp_ref, pv0_ref, pv1_ref, x_ref),
    ):
        pool[0:S, :] = first[...]
        pool[S:ROWS, :] = second[...]
        pool[ROWS : 2 * ROWS, :] = own[...]
    parts = []
    for i in range(FR_DEV):
        span = slice(i * S, (i + 1) * S)
        other = pl.ds(pl.multiple_of(t_ref[i] * S, S), S)
        q = q_ref[span, :]
        g = g_ref[span, :]
        keys = jnp.concatenate([k_ref[span, :], kp_ref[other, :], sk_ref[...]], axis=0)
        values = jnp.concatenate([x_ref[span, :], vp_ref[other, :], sv_ref[...]], axis=0)
        scores = mm_nt(q, keys) * scale
        powers = jnp.exp(scores - jnp.max(scores, axis=1, keepdims=True))
        probs = powers * (1.0 / jnp.sum(powers, axis=1, keepdims=True))
        probs_b = probs.astype(BF16)
        out = mm(probs_b, values)
        delta = jnp.sum(g.astype(F32) * out, axis=1, keepdims=True)
        dscores = (probs * (mm_nt(g, values) - delta)).astype(BF16)
        gq_ref[span, :] = (mm(dscores, keys) * scale).astype(BF16)
        parts.append((mm_tn(dscores, q) * scale, mm_tn(probs_b, g)))
    hits = [[(t_ref[i] == j).astype(F32) for j in range(2 * FR_DEV)] for i in range(FR_DEV)]
    for c, (own_ref, back_ref) in enumerate(((ok_ref, rk_ref), (ov_ref, rv_ref))):
        others = [parts[i][c][S : 2 * S] for i in range(FR_DEV)]
        for j in range(FR_DEV):
            span = slice(j * S, (j + 1) * S)
            back_ref[span, :] = (hits[0][j] * others[0] + hits[1][j] * others[1]).astype(BF16)
            own_ref[span, :] = (
                parts[j][c][:S]
                + hits[0][FR_DEV + j] * others[0]
                + hits[1][FR_DEV + j] * others[1]
            )
        sink_ref[c * S : (c + 1) * S, :] = parts[0][c][2 * S :] + parts[1][c][2 * S :]


def entering_kernel(
    cum_ref, x_ref, g_ref, b_ref, c_ref, dx_ref, sp_ref, gp_ref, si_ref, gi_ref,
    gbl_ref, gcl_ref, ssm_ref, gb_ref, gc_ref,
):
    @pl.when(pl.program_id(0) == 0)
    def _():
        gb_ref[...] = gbl_ref[...]
        gc_ref[...] = gcl_ref[...]

    _, blocks = decay_terms(cum_ref)
    state_in = si_ref[...].astype(F32)
    grad_in = gi_ref[...].astype(F32)
    befores = [state_in, blocks[0][4] * state_in + sp_ref[...]]
    afters = [gp_ref[...] + blocks[1][4] * grad_in, grad_in]
    for b in range(FR_DEV):
        span = slice(b * S, (b + 1) * S)
        _, _, to_end, grown, _ = blocks[b]
        after = afters[b].astype(BF16)
        before = befores[b].astype(BF16)
        x_scaled = (x_ref[span, :].astype(F32) * to_end).astype(BF16)
        g_scaled = (g_ref[span, :].astype(F32) * grown).astype(BF16)
        gb_ref[span, :] += mm(x_scaled, after)
        gc_ref[span, :] += mm(g_scaled, before)
        ssm_ref[span, :] = dx_ref[span, :] + to_end * mm_nt(b_ref[span, :], after)


def sum_kernel(
    own_ref, ssm_ref, ok_ref, ov_ref, k0_ref, v0_ref, k1_ref, v1_ref, sk_ref, sv_ref,
    gin_ref, gk_ref,
):
    first = pl.program_id(0) < pl.num_programs(0) // 2

    def add(k_ref, v_ref):
        for b in range(FR_DEV):
            span = slice(b * S, (b + 1) * S)
            mine = (own_ref[0] == b).astype(F32)
            gin_ref[span, :] = (
                ssm_ref[span, :]
                + ov_ref[span, :]
                + v_ref[span, :].astype(F32)
                + mine * sv_ref[...].astype(F32)
            ).astype(BF16)
            gk_ref[span, :] = (
                ok_ref[span, :]
                + k_ref[span, :].astype(F32)
                + mine * sk_ref[...].astype(F32)
            ).astype(BF16)

    @pl.when(first)
    def _():
        add(k0_ref, v0_ref)

    @pl.when(jnp.logical_not(first))
    def _():
        add(k1_ref, v1_ref)


def swap(value, axis, bit):
    return lax.ppermute(value, axis, [(i, i ^ bit) for i in range(lax.axis_size(axis))])


def beside(value, waiting, done):
    if not waiting:
        return value
    value, arrived = lax.optimization_barrier((value, waiting.pop(0)))
    done.append(arrived)
    return value


def halve(value, axis, bit, stop, waiting=(), done=()):
    place = lax.axis_index(axis)
    while bit < stop:
        high = (place // bit) % 2
        half = value.shape[0] // 2
        keep = lax.dynamic_slice_in_dim(value, high * half, half)
        give = lax.dynamic_slice_in_dim(value, (1 - high) * half, half)
        value = keep + swap(give.astype(BF16), axis, bit).astype(value.dtype)
        value = beside(value, waiting, done)
        bit *= 2
    return value


def double(value, axis, waiting=(), done=()):
    place = lax.axis_index(axis)
    bit = lax.axis_size(axis) // 2
    while bit:
        high = (place // bit) % 2 == 1
        got = swap(value, axis, bit)
        value = jnp.concatenate([jnp.where(high, got, value), jnp.where(high, value, got)])
        value = beside(value, waiting, done)
        bit //= 2
    return value


def shift(value, axis, by):
    peers = lax.axis_size(axis)
    return lax.ppermute(
        value, axis, [(i, i + by) for i in range(peers) if 0 <= i + by < peers]
    )


def shards(
    mixer_input, state_input, state_output, log_decay, queries, attn_keys, out_grad,
    frame_offsets, sink_frame_index,
):
    peers = lax.axis_size("frame")
    device = lax.axis_index("frame")
    first_frame = device * FR_DEV
    params = pltpu.CompilerParams(vmem_limit_bytes=40 * 1024 * 1024)

    cols = pl.BlockSpec((ROWS, 128), lambda a, *_: (0, a))
    frame_lo = pl.BlockSpec((S, 128), lambda a, *_: (0, a))
    frame_hi = pl.BlockSpec((S, 128), lambda a, *_: (1, a))
    state = pl.BlockSpec((128, NSTATE), lambda a, *_: (a, 0))
    fixed = pl.BlockSpec((ROWS, NSTATE), lambda a, *_: (0, 0))
    cum_spec = pl.BlockSpec((1, 8, ROWS), lambda a, *_: (a, 0, 0))
    wide = lambda dtype: jax.ShapeDtypeStruct((ROWS, DI), dtype)
    tall = lambda dtype: jax.ShapeDtypeStruct((DI, NSTATE), dtype)
    small = jax.ShapeDtypeStruct((ROWS, NSTATE), F32)

    behind = [
        shift(a[i * S : (i + 1) * S], "frame", 1)
        for a in (attn_keys, mixer_input)
        for i in range(FR_DEV)
    ]
    sink_index = sink_frame_index[0]
    sink_owner = sink_index // FR_DEV
    sink_slot = sink_index % FR_DEV
    picked = jnp.concatenate(
        [
            lax.dynamic_slice_in_dim(attn_keys, sink_slot * S, S),
            lax.dynamic_slice_in_dim(mixer_input, sink_slot * S, S),
        ]
    )
    picked = jnp.where(device == sink_owner, picked, jnp.zeros_like(picked))
    sink_part = halve(picked, "frame", 1, 2)

    before = jnp.triu(jnp.ones((S, S), F32))
    cumulative = jnp.einsum(
        "bsh,st->hbt",
        log_decay.reshape(FR_DEV, S, HEADS),
        before,
        precision=lax.Precision.HIGHEST,
    )
    total = jnp.exp(jnp.sum(cumulative[:, :, -1], axis=1))
    cum_rows = cumulative.reshape(GROUPS, 2, ROWS)
    cum_rows = jnp.pad(cum_rows, ((0, 0), (0, 6), (0, 0)))
    dx, sp, gp, local_state, local_grad, gb_local, gc_local = pl.pallas_call(
        local_kernel,
        grid=(GROUPS,),
        in_specs=[cum_spec, cols, cols, fixed, fixed],
        out_specs=[cols, state, state, state, state, fixed, fixed],
        out_shape=[wide(F32), tall(F32), tall(F32), tall(BF16), tall(BF16), small, small],
        scratch_shapes=[pltpu.VMEM((FR_DEV, S, S), F32), pltpu.VMEM((FR_DEV, S, S), F32)],
        compiler_params=params,
        cost_estimate=pl.CostEstimate(
            flops=1_000_000_000, bytes_accessed=10_000_000, transcendentals=1_500_000
        ),
    )(cum_rows, mixer_input, out_grad, state_input, state_output)

    heads = HEADS // peers
    rows = DI // peers
    high = total.astype(BF16)
    rest = total - high.astype(F32)
    mid = rest.astype(BF16)
    low = (rest - mid.astype(F32)).astype(BF16)
    decay_rows = jnp.stack([high, mid, low], axis=-1).reshape(peers, heads * 3, 1)
    decay_rows = jnp.pad(decay_rows, ((0, 0), (0, 16 - heads * 3), (0, 0)))
    decay_rows = jnp.broadcast_to(decay_rows, (peers, 16, NSTATE))
    sent = jnp.concatenate(
        [
            local_state.reshape(peers, rows, NSTATE),
            local_grad.reshape(peers, rows, NSTATE),
            decay_rows,
        ],
        axis=1,
    )
    sink_part, sent, early = lax.optimization_barrier((sink_part, sent, behind[:2]))
    waiting = behind[2:] + [lax.all_to_all(sent, "frame", 0, 0)]
    done = []
    sink_part = halve(sink_part, "frame", 2, peers, waiting, done)
    sink_pair = double(sink_part, "frame", waiting, done)
    behind, got = list(early) + done[:2], done[2]
    scanned = pl.pallas_call(
        lambda *refs: scan_kernel(heads, rows, *refs),
        out_shape=jax.ShapeDtypeStruct((peers, 2 * rows, NSTATE), BF16),
        compiler_params=params,
    )(got)
    scanned, sink_pair = lax.optimization_barrier((scanned, sink_pair))
    entered = lax.all_to_all(scanned, "frame", 0, 0)

    frame_ids = first_frame + jnp.arange(FR_DEV, dtype=jnp.int32)
    own_offsets = lax.dynamic_slice_in_dim(frame_offsets, first_frame, FR_DEV)
    target = jnp.maximum(frame_ids - own_offsets, 0) - first_frame + OFFMAX
    halves = GROUPS // 2

    def attend(first_group, earlier):
        part = pl.BlockSpec((ROWS, 128), lambda a, *_: (0, a + first_group))
        part_lo = pl.BlockSpec((S, 128), lambda a, *_: (0, a + first_group))
        part_hi = pl.BlockSpec((S, 128), lambda a, *_: (1, a + first_group))
        half = jax.ShapeDtypeStruct((ROWS, DI // 2), BF16)
        return pl.pallas_call(
            attn_kernel,
            grid_spec=pltpu.PrefetchScalarGridSpec(
                num_scalar_prefetch=1,
                grid=(halves,),
                in_specs=[part] * 4
                + [part_lo] * 5
                + [part_hi]
                + [pl.BlockSpec(memory_space=pl.ANY)] * len(earlier),
                out_specs=[part] * 4 + [cols] * 2,
                scratch_shapes=[
                    pltpu.VMEM((2 * ROWS, 128), BF16),
                    pltpu.VMEM((2 * ROWS, 128), BF16),
                ],
            ),
            out_shape=[wide(BF16), wide(F32), wide(F32), wide(F32), half, half],
            input_output_aliases={11 + i: i for i in range(len(earlier))},
            compiler_params=params,
            cost_estimate=pl.CostEstimate(
                flops=1_500_000_000, bytes_accessed=7_000_000, transcendentals=800_000
            ),
        )(
            target, queries, attn_keys, mixer_input, out_grad, *behind, sink_pair, sink_pair,
            *earlier,
        )

    *earlier, back_k0, back_v0 = attend(0, ())
    grad_q, own_k, own_v, sink_terms, back_k1, back_v1 = attend(halves, tuple(earlier))

    returned_k0 = shift(back_k0, "frame", -1)
    entered, sink_terms, returned_k0, back_v0, back_k1, back_v1 = lax.optimization_barrier(
        (entered, sink_terms, returned_k0, back_v0, back_k1, back_v1)
    )
    state_in = entered[:, :rows].reshape(DI, NSTATE)
    grad_in = entered[:, rows:].reshape(DI, NSTATE)
    ssm, grad_b, grad_c = pl.pallas_call(
        entering_kernel,
        grid=(GROUPS,),
        in_specs=[cum_spec, cols, cols, fixed, fixed, cols, state, state, state, state]
        + [fixed, fixed],
        out_specs=[cols, fixed, fixed],
        out_shape=[wide(F32), small, small],
        compiler_params=params,
        cost_estimate=pl.CostEstimate(
            flops=600_000_000, bytes_accessed=12_000_000, transcendentals=1_000_000
        ),
    )(
        cum_rows, mixer_input, out_grad, state_input, state_output, dx, sp, gp,
        state_in, grad_in, gb_local, gc_local,
    )
    returned_v0, returned_k1, returned_v1 = [
        shift(a, "frame", -1) for a in (back_v0, back_k1, back_v1)
    ]
    waiting = [(ssm, returned_v0), returned_k1, returned_v1]
    done = []
    sink_part = halve(sink_terms, "frame", 1, peers, waiting, done)
    sink_grads = double(sink_part.astype(BF16), "frame")
    (ssm, returned_v0), returned_k1, returned_v1 = done
    owned = jnp.where(device == sink_owner, sink_slot, -1).astype(jnp.int32).reshape(1)

    pair = pl.BlockSpec((ROWS, 256), lambda a, *_: (0, a))
    steps = DI // 256
    left = pl.BlockSpec((ROWS, 256), lambda a, *_: (0, jnp.minimum(a, steps // 2 - 1)))
    right = pl.BlockSpec((ROWS, 256), lambda a, *_: (0, jnp.maximum(a - steps // 2, 0)))
    pair_lo = pl.BlockSpec((S, 256), lambda a, *_: (0, a))
    pair_hi = pl.BlockSpec((S, 256), lambda a, *_: (1, a))
    grad_input, grad_keys = pl.pallas_call(
        sum_kernel,
        grid_spec=pltpu.PrefetchScalarGridSpec(
            num_scalar_prefetch=1,
            grid=(steps,),
            in_specs=[pair, pair, pair, left, left, right, right, pair_lo, pair_hi],
            out_specs=[pair, pair],
        ),
        out_shape=[wide(BF16), wide(BF16)],
        compiler_params=params,
    )(
        owned, ssm, own_k, own_v, returned_k0, returned_v0, returned_k1, returned_v1,
        sink_grads, sink_grads,
    )
    return (grad_input, grad_q, grad_keys, grad_b, grad_c)


def solution(mesh):
    rows = P(("grp", "frame"), None)
    return jax.shard_map(
        shards,
        mesh=mesh,
        in_specs=(rows,) * 7 + (P("grp"), P("grp")),
        out_specs=(rows,) * 5,
        check_vma=False,
    )
```

```python
import jax
import jax.numpy as jnp
from jax import lax
from jax.experimental import pallas as pl
from jax.experimental.pallas import tpu as pltpu
from jax.sharding import PartitionSpec as P

DI = 2048
HEADDIM = 64
NSTATE = 128
ATTENTION_WIDTH = 128
S = 128
FR_DEV = 2
OFFMAX = 2
HEADS = DI // HEADDIM
GROUPS = DI // 128
ROWS = FR_DEV * S
F32 = jnp.float32
BF16 = jnp.bfloat16


def mm(a, b):
    return lax.dot_general(a, b, (((1,), (0,)), ((), ())), preferred_element_type=F32)


def mm_nt(a, b):
    return lax.dot_general(a, b, (((1,), (1,)), ((), ())), preferred_element_type=F32)


def mm_tn(a, b):
    return lax.dot_general(a, b, (((0,), (0,)), ((), ())), preferred_element_type=F32)


def decay_terms(cum_ref):
    rows = cum_ref[0]
    cols = jnp.transpose(rows)
    lane = lax.broadcasted_iota(jnp.int32, (S, 128), 1) < HEADDIM
    sub = lax.broadcasted_iota(jnp.int32, (128, NSTATE), 0) < HEADDIM
    blocks = []
    for b in range(FR_DEV):
        span = slice(b * S, (b + 1) * S)
        row = [rows[j : j + 1, span] for j in range(2)]
        col = [cols[span, j : j + 1] for j in range(2)]
        end = [r[:, S - 1 : S] for r in row]
        to_end = jnp.where(lane, jnp.exp(end[0] - col[0]), jnp.exp(end[1] - col[1]))
        grown = jnp.where(lane, jnp.exp(col[0]), jnp.exp(col[1]))
        whole = jnp.where(sub, jnp.exp(end[0]), jnp.exp(end[1]))
        blocks.append((row, col, to_end, grown, whole))
    return lane, blocks


def local_kernel(
    cum_ref, x_ref, g_ref, b_ref, c_ref,
    dx_ref, sp_ref, gp_ref, ls_ref, lg_ref, gb_ref, gc_ref,
    cb_ref, fold_ref,
):
    step = pl.program_id(0)

    @pl.when(step == 0)
    def _():
        for b in range(FR_DEV):
            span = slice(b * S, (b + 1) * S)
            cb_ref[b] = mm_nt(b_ref[span, :], c_ref[span, :])
            fold_ref[b] = jnp.zeros((S, S), F32)

    lane, blocks = decay_terms(cum_ref)
    causal = lax.broadcasted_iota(jnp.int32, (S, S), 0) <= lax.broadcasted_iota(
        jnp.int32, (S, S), 1
    )
    states, grads = [], []
    for b in range(FR_DEV):
        span = slice(b * S, (b + 1) * S)
        row, col, to_end, grown, whole = blocks[b]
        x = x_ref[span, :]
        g = g_ref[span, :]
        xf = x.astype(F32)
        inner, folded = [], None
        for j in range(2):
            weights = jnp.exp(jnp.where(causal, row[j] - col[j], -1e30))
            mixing = (weights * cb_ref[b]).astype(BF16)
            x_head = jnp.where(lane if j == 0 else ~lane, xf, 0.0).astype(BF16)
            term = weights * mm_nt(x_head, g)
            folded = term if folded is None else folded + term
            inner.append(mm(mixing, g))
        fold_ref[b] += folded
        dx_ref[span, :] = jnp.where(lane, inner[0], inner[1])
        x_scaled = (xf * to_end).astype(BF16)
        g_scaled = (g.astype(F32) * grown).astype(BF16)
        states.append(mm_tn(x_scaled, b_ref[span, :]))
        grads.append(mm_tn(g_scaled, c_ref[span, :]))
    sp_ref[...] = states[0]
    gp_ref[...] = grads[1]
    ls_ref[...] = (blocks[1][4] * states[0] + states[1]).astype(BF16)
    lg_ref[...] = (grads[0] + blocks[0][4] * grads[1]).astype(BF16)

    @pl.when(step == GROUPS - 1)
    def _():
        for b in range(FR_DEV):
            span = slice(b * S, (b + 1) * S)
            folded_b = fold_ref[b].astype(BF16)
            gb_ref[span, :] = mm(folded_b, c_ref[span, :])
            gc_ref[span, :] = mm_tn(folded_b, b_ref[span, :])


def scan_kernel(heads, rows, in_ref, out_ref):
    count = in_ref.shape[0]
    decays = []
    for d in range(count):
        tail = in_ref[d, 2 * rows :, :].astype(F32)
        decays.append(tail)
    for j in range(heads):
        for back in range(2):
            lo = back * rows + j * HEADDIM
            carry = jnp.zeros((HEADDIM, NSTATE), F32)
            for turn in range(count):
                d = count - 1 - turn if back else turn
                out_ref[d, lo : lo + HEADDIM, :] = carry.astype(BF16)
                decay = (
                    decays[d][3 * j : 3 * j + 1, :]
                    + decays[d][3 * j + 1 : 3 * j + 2, :]
                    + decays[d][3 * j + 2 : 3 * j + 3, :]
                )
                carry = decay * carry + in_ref[d, lo : lo + HEADDIM, :].astype(F32)


def attn_kernel(
    t_ref, q_ref, k_ref, x_ref, g_ref, pk0_ref, pk1_ref, pv0_ref, pv1_ref, sk_ref, sv_ref,
    *refs,
):
    gq_ref, ok_ref, ov_ref, sink_ref, rk_ref, rv_ref, kp_ref, vp_ref = refs[-8:]
    scale = ATTENTION_WIDTH ** (-0.5)
    for pool, first, second, own in (
        (kp_ref, pk0_ref, pk1_ref, k_ref),
        (vp_ref, pv0_ref, pv1_ref, x_ref),
    ):
        pool[0:S, :] = first[...]
        pool[S:ROWS, :] = second[...]
        pool[ROWS : 2 * ROWS, :] = own[...]
    parts = []
    for i in range(FR_DEV):
        span = slice(i * S, (i + 1) * S)
        other = pl.ds(pl.multiple_of(t_ref[i] * S, S), S)
        q = q_ref[span, :]
        g = g_ref[span, :]
        keys = jnp.concatenate([k_ref[span, :], kp_ref[other, :], sk_ref[...]], axis=0)
        values = jnp.concatenate([x_ref[span, :], vp_ref[other, :], sv_ref[...]], axis=0)
        scores = mm_nt(q, keys) * scale
        powers = jnp.exp(scores - jnp.max(scores, axis=1, keepdims=True))
        probs = powers * (1.0 / jnp.sum(powers, axis=1, keepdims=True))
        probs_b = probs.astype(BF16)
        out = mm(probs_b, values)
        delta = jnp.sum(g.astype(F32) * out, axis=1, keepdims=True)
        dscores = (probs * (mm_nt(g, values) - delta)).astype(BF16)
        gq_ref[span, :] = (mm(dscores, keys) * scale).astype(BF16)
        parts.append((mm_tn(dscores, q) * scale, mm_tn(probs_b, g)))
    hits = [[(t_ref[i] == j).astype(F32) for j in range(2 * FR_DEV)] for i in range(FR_DEV)]
    for c, (own_ref, back_ref) in enumerate(((ok_ref, rk_ref), (ov_ref, rv_ref))):
        others = [parts[i][c][S : 2 * S] for i in range(FR_DEV)]
        for j in range(FR_DEV):
            span = slice(j * S, (j + 1) * S)
            back_ref[span, :] = (hits[0][j] * others[0] + hits[1][j] * others[1]).astype(BF16)
            own_ref[span, :] = (
                parts[j][c][:S]
                + hits[0][FR_DEV + j] * others[0]
                + hits[1][FR_DEV + j] * others[1]
            )
        sink_ref[c * S : (c + 1) * S, :] = parts[0][c][2 * S :] + parts[1][c][2 * S :]


def entering_kernel(
    cum_ref, x_ref, g_ref, b_ref, c_ref, dx_ref, sp_ref, gp_ref, si_ref, gi_ref,
    gbl_ref, gcl_ref, ssm_ref, gb_ref, gc_ref,
):
    @pl.when(pl.program_id(0) == 0)
    def _():
        gb_ref[...] = gbl_ref[...]
        gc_ref[...] = gcl_ref[...]

    _, blocks = decay_terms(cum_ref)
    state_in = si_ref[...].astype(F32)
    grad_in = gi_ref[...].astype(F32)
    befores = [state_in, blocks[0][4] * state_in + sp_ref[...]]
    afters = [gp_ref[...] + blocks[1][4] * grad_in, grad_in]
    for b in range(FR_DEV):
        span = slice(b * S, (b + 1) * S)
        _, _, to_end, grown, _ = blocks[b]
        after = afters[b].astype(BF16)
        before = befores[b].astype(BF16)
        x_scaled = (x_ref[span, :].astype(F32) * to_end).astype(BF16)
        g_scaled = (g_ref[span, :].astype(F32) * grown).astype(BF16)
        gb_ref[span, :] += mm(x_scaled, after)
        gc_ref[span, :] += mm(g_scaled, before)
        ssm_ref[span, :] = dx_ref[span, :] + to_end * mm_nt(b_ref[span, :], after)


def sum_kernel(
    own_ref, ssm_ref, ok_ref, ov_ref, k0_ref, v0_ref, k1_ref, v1_ref, sk_ref, sv_ref,
    gin_ref, gk_ref,
):
    first = pl.program_id(0) < pl.num_programs(0) // 2

    def add(k_ref, v_ref):
        for b in range(FR_DEV):
            span = slice(b * S, (b + 1) * S)
            mine = (own_ref[0] == b).astype(F32)
            gin_ref[span, :] = (
                ssm_ref[span, :]
                + ov_ref[span, :]
                + v_ref[span, :].astype(F32)
                + mine * sv_ref[...].astype(F32)
            ).astype(BF16)
            gk_ref[span, :] = (
                ok_ref[span, :]
                + k_ref[span, :].astype(F32)
                + mine * sk_ref[...].astype(F32)
            ).astype(BF16)

    @pl.when(first)
    def _():
        add(k0_ref, v0_ref)

    @pl.when(jnp.logical_not(first))
    def _():
        add(k1_ref, v1_ref)


def swap(value, axis, bit):
    return lax.ppermute(value, axis, [(i, i ^ bit) for i in range(lax.axis_size(axis))])


def beside(value, waiting, done):
    if not waiting:
        return value
    value, arrived = lax.optimization_barrier((value, waiting.pop(0)))
    done.append(arrived)
    return value


def halve(value, axis, bit, stop, waiting=(), done=()):
    place = lax.axis_index(axis)
    while bit < stop:
        high = (place // bit) % 2
        half = value.shape[0] // 2
        keep = lax.dynamic_slice_in_dim(value, high * half, half)
        give = lax.dynamic_slice_in_dim(value, (1 - high) * half, half)
        value = keep + swap(give.astype(BF16), axis, bit).astype(value.dtype)
        value = beside(value, waiting, done)
        bit *= 2
    return value


def double(value, axis, waiting=(), done=()):
    place = lax.axis_index(axis)
    bit = lax.axis_size(axis) // 2
    while bit:
        high = (place // bit) % 2 == 1
        got = swap(value, axis, bit)
        value = jnp.concatenate([jnp.where(high, got, value), jnp.where(high, value, got)])
        value = beside(value, waiting, done)
        bit //= 2
    return value


def shift(value, axis, by):
    peers = lax.axis_size(axis)
    return lax.ppermute(
        value, axis, [(i, i + by) for i in range(peers) if 0 <= i + by < peers]
    )


def shards(
    mixer_input, state_input, state_output, log_decay, queries, attn_keys, out_grad,
    frame_offsets, sink_frame_index,
):
    peers = lax.axis_size("frame")
    device = lax.axis_index("frame")
    first_frame = device * FR_DEV
    params = pltpu.CompilerParams(vmem_limit_bytes=40 * 1024 * 1024)

    cols = pl.BlockSpec((ROWS, 128), lambda a, *_: (0, a))
    frame_lo = pl.BlockSpec((S, 128), lambda a, *_: (0, a))
    frame_hi = pl.BlockSpec((S, 128), lambda a, *_: (1, a))
    state = pl.BlockSpec((128, NSTATE), lambda a, *_: (a, 0))
    fixed = pl.BlockSpec((ROWS, NSTATE), lambda a, *_: (0, 0))
    cum_spec = pl.BlockSpec((1, 8, ROWS), lambda a, *_: (a, 0, 0))
    wide = lambda dtype: jax.ShapeDtypeStruct((ROWS, DI), dtype)
    tall = lambda dtype: jax.ShapeDtypeStruct((DI, NSTATE), dtype)
    small = jax.ShapeDtypeStruct((ROWS, NSTATE), F32)

    behind = [
        shift(a[i * S : (i + 1) * S], "frame", 1)
        for a in (attn_keys, mixer_input)
        for i in range(FR_DEV)
    ]
    sink_index = sink_frame_index[0]
    sink_owner = sink_index // FR_DEV
    sink_slot = sink_index % FR_DEV
    picked = jnp.concatenate(
        [
            lax.dynamic_slice_in_dim(attn_keys, sink_slot * S, S),
            lax.dynamic_slice_in_dim(mixer_input, sink_slot * S, S),
        ]
    )
    picked = jnp.where(device == sink_owner, picked, jnp.zeros_like(picked))
    sink_part = halve(picked, "frame", 1, 2)

    before = jnp.triu(jnp.ones((S, S), F32))
    cumulative = jnp.einsum(
        "bsh,st->hbt",
        log_decay.reshape(FR_DEV, S, HEADS),
        before,
        precision=lax.Precision.HIGHEST,
    )
    total = jnp.exp(jnp.sum(cumulative[:, :, -1], axis=1))
    cum_rows = cumulative.reshape(GROUPS, 2, ROWS)
    cum_rows = jnp.pad(cum_rows, ((0, 0), (0, 6), (0, 0)))
    dx, sp, gp, local_state, local_grad, gb_local, gc_local = pl.pallas_call(
        local_kernel,
        grid=(GROUPS,),
        in_specs=[cum_spec, cols, cols, fixed, fixed],
        out_specs=[cols, state, state, state, state, fixed, fixed],
        out_shape=[wide(F32), tall(F32), tall(F32), tall(BF16), tall(BF16), small, small],
        scratch_shapes=[pltpu.VMEM((FR_DEV, S, S), F32), pltpu.VMEM((FR_DEV, S, S), F32)],
        compiler_params=params,
        cost_estimate=pl.CostEstimate(
            flops=1_000_000_000, bytes_accessed=10_000_000, transcendentals=1_500_000
        ),
    )(cum_rows, mixer_input, out_grad, state_input, state_output)

    heads = HEADS // peers
    rows = DI // peers
    high = total.astype(BF16)
    rest = total - high.astype(F32)
    mid = rest.astype(BF16)
    low = (rest - mid.astype(F32)).astype(BF16)
    decay_rows = jnp.stack([high, mid, low], axis=-1).reshape(peers, heads * 3, 1)
    decay_rows = jnp.pad(decay_rows, ((0, 0), (0, 16 - heads * 3), (0, 0)))
    decay_rows = jnp.broadcast_to(decay_rows, (peers, 16, NSTATE))
    sent = jnp.concatenate(
        [
            local_state.reshape(peers, rows, NSTATE),
            local_grad.reshape(peers, rows, NSTATE),
            decay_rows,
        ],
        axis=1,
    )
    sink_part, sent, early = lax.optimization_barrier((sink_part, sent, behind[:2]))
    waiting = behind[2:]
    done = []
    sink_part = halve(sink_part, "frame", 2, peers, waiting, done)
    sink_pair = double(sink_part, "frame", waiting, done)
    behind = list(early) + done
    sent, sink_pair = lax.optimization_barrier((sent, sink_pair))
    got = lax.all_to_all(sent, "frame", 0, 0)
    frame_ids = first_frame + jnp.arange(FR_DEV, dtype=jnp.int32)
    own_offsets = lax.dynamic_slice_in_dim(frame_offsets, first_frame, FR_DEV)
    target = jnp.maximum(frame_ids - own_offsets, 0) - first_frame + OFFMAX
    halves = GROUPS // 2

    def attend(first_group, earlier):
        part = pl.BlockSpec((ROWS, 128), lambda a, *_: (0, a + first_group))
        part_lo = pl.BlockSpec((S, 128), lambda a, *_: (0, a + first_group))
        part_hi = pl.BlockSpec((S, 128), lambda a, *_: (1, a + first_group))
        half = jax.ShapeDtypeStruct((ROWS, DI // 2), BF16)
        return pl.pallas_call(
            attn_kernel,
            grid_spec=pltpu.PrefetchScalarGridSpec(
                num_scalar_prefetch=1,
                grid=(halves,),
                in_specs=[part] * 4
                + [part_lo] * 5
                + [part_hi]
                + [pl.BlockSpec(memory_space=pl.ANY)] * len(earlier),
                out_specs=[part] * 4 + [cols] * 2,
                scratch_shapes=[
                    pltpu.VMEM((2 * ROWS, 128), BF16),
                    pltpu.VMEM((2 * ROWS, 128), BF16),
                ],
            ),
            out_shape=[wide(BF16), wide(F32), wide(F32), wide(F32), half, half],
            input_output_aliases={11 + i: i for i in range(len(earlier))},
            compiler_params=params,
            cost_estimate=pl.CostEstimate(
                flops=1_500_000_000, bytes_accessed=7_000_000, transcendentals=800_000
            ),
        )(
            target, queries, attn_keys, mixer_input, out_grad, *behind, sink_pair, sink_pair,
            *earlier,
        )

    *earlier, back_k0, back_v0 = attend(0, ())
    got, earlier = lax.optimization_barrier((got, earlier))
    scanned = pl.pallas_call(
        lambda *refs: scan_kernel(heads, rows, *refs),
        out_shape=jax.ShapeDtypeStruct((peers, 2 * rows, NSTATE), BF16),
        compiler_params=params,
    )(got)
    scanned, earlier = lax.optimization_barrier((scanned, earlier))
    entered = lax.all_to_all(scanned, "frame", 0, 0)
    grad_q, own_k, own_v, sink_terms, back_k1, back_v1 = attend(halves, tuple(earlier))

    returned_k0 = shift(back_k0, "frame", -1)
    entered, sink_terms, returned_k0, back_v0, back_k1, back_v1 = lax.optimization_barrier(
        (entered, sink_terms, returned_k0, back_v0, back_k1, back_v1)
    )
    state_in = entered[:, :rows].reshape(DI, NSTATE)
    grad_in = entered[:, rows:].reshape(DI, NSTATE)
    ssm, grad_b, grad_c = pl.pallas_call(
        entering_kernel,
        grid=(GROUPS,),
        in_specs=[cum_spec, cols, cols, fixed, fixed, cols, state, state, state, state]
        + [fixed, fixed],
        out_specs=[cols, fixed, fixed],
        out_shape=[wide(F32), small, small],
        compiler_params=params,
        cost_estimate=pl.CostEstimate(
            flops=600_000_000, bytes_accessed=12_000_000, transcendentals=1_000_000
        ),
    )(
        cum_rows, mixer_input, out_grad, state_input, state_output, dx, sp, gp,
        state_in, grad_in, gb_local, gc_local,
    )
    returned_v0, returned_k1, returned_v1 = [
        shift(a, "frame", -1) for a in (back_v0, back_k1, back_v1)
    ]
    waiting = [(ssm, returned_v0), returned_k1, returned_v1]
    done = []
    sink_part = halve(sink_terms, "frame", 1, peers, waiting, done)
    sink_grads = double(sink_part.astype(BF16), "frame")
    (ssm, returned_v0), returned_k1, returned_v1 = done
    owned = jnp.where(device == sink_owner, sink_slot, -1).astype(jnp.int32).reshape(1)

    pair = pl.BlockSpec((ROWS, 256), lambda a, *_: (0, a))
    steps = DI // 256
    left = pl.BlockSpec((ROWS, 256), lambda a, *_: (0, jnp.minimum(a, steps // 2 - 1)))
    right = pl.BlockSpec((ROWS, 256), lambda a, *_: (0, jnp.maximum(a - steps // 2, 0)))
    pair_lo = pl.BlockSpec((S, 256), lambda a, *_: (0, a))
    pair_hi = pl.BlockSpec((S, 256), lambda a, *_: (1, a))
    grad_input, grad_keys = pl.pallas_call(
        sum_kernel,
        grid_spec=pltpu.PrefetchScalarGridSpec(
            num_scalar_prefetch=1,
            grid=(steps,),
            in_specs=[pair, pair, pair, left, left, right, right, pair_lo, pair_hi],
            out_specs=[pair, pair],
        ),
        out_shape=[wide(BF16), wide(BF16)],
        compiler_params=params,
    )(
        owned, ssm, own_k, own_v, returned_k0, returned_v0, returned_k1, returned_v1,
        sink_grads, sink_grads,
    )
    return (grad_input, grad_q, grad_keys, grad_b, grad_c)


def solution(mesh):
    rows = P(("grp", "frame"), None)
    return jax.shard_map(
        shards,
        mesh=mesh,
        in_specs=(rows,) * 7 + (P("grp"), P("grp")),
        out_specs=(rows,) * 5,
        check_vma=False,
    )
```
